32 devices in a mesh: dp: 2 (over x), row: 4 (over y, core), col: 4 (over z).
Axes of the slice: x: 2, y: 2, z: 4, core: 2. Of those that a mesh axis runs over, the one named last changes fastest.
Arguments:
- tokens: bfloat16 [4096, 8192], P(('dp', 'row', 'col')), parts along dimension 0, may hold values from -60 to 60
- norm_gain: float32 [8192], replicated, may hold values from 0.1 to 1.9
- w_key: bfloat16 [8192, 1024], P('row', 'col'), may hold values from -0.0625 to 0.0625
- w_value: bfloat16 [8192, 1024], P('row', 'col'), may hold values from -0.0625 to 0.0625
Outputs:
- key_rows: bfloat16 [4096, 1024], P(('dp', 'row', 'col')), parts along dimension 0
- value_rows: bfloat16 [4096, 1024], P(('dp', 'row', 'col')), parts along dimension 0
The draws below stay inside these ranges and needn't reach their ends.
There are 2 independent parts, one for each index of `dp`. The reference program is written for one: setup_inputs(seed, part) draws one part's arguments, and reference() takes and returns one part's arrays. A program takes and returns all parts, laid end to end along the dimension named above; an argument that names none is the same for every part. Nothing has to cross between parts.
All inputs are finite; a program needn't handle non-finite values.
Results may differ from the reference program's by a relative error of at most 0.014.
Values may be sent and summed in bfloat16 or wider, within the bound.
No kernel may reach another device: no remote copies, remote signals or barrier semaphores. Data moves between devices by JAX's collectives and lax.ppermute only.
A program may use at most 64 MiB of HBM per device.

```python
import jax
import jax.numpy as jnp
from jax import lax

D = 8192
HEAD = 128
KVW = 1024
LEN = 2048
N_ROW = 4


def draw_tokens(key, part):
    key_base = jax.random.fold_in(key, 11)
    key_rows = jax.random.fold_in(key, 12)
    key_cols = jax.random.fold_in(key, 13)
    row_scales = jnp.exp(jax.random.uniform(key_rows, (LEN, 1), jnp.float32, -1.2, 1.2))
    col_scales = jnp.exp(jax.random.uniform(key_cols, (1, D), jnp.float32, -1.2, 1.2))
    entries = jnp.clip(jax.random.normal(key_base, (LEN, D), jnp.float32), -5.0, 5.0)
    return (entries * row_scales * col_scales).astype(jnp.bfloat16)


def levels(stream_key, dims, cuts, smallest, top_value):
    def one(dim, blocks):
        heights = jax.random.uniform(jax.random.fold_in(jax.random.fold_in(stream_key, 6), dim), (blocks,), jnp.float32, smallest / len(cuts), top_value / len(cuts))
        return jnp.repeat(jnp.exp(heights), dims[dim] // blocks).reshape((-1,) + (1,) * (len(dims) - dim - 1))

    level = one(*cuts[0])
    for cut in cuts[1:]:
        level = level * one(*cut)
    return level


def centred(stream_key, dims, scale, bound, split=(), kind=jnp.bfloat16):
    level = levels(stream_key, dims, split, -0.22, 0.18) if split else 1.0
    values = jax.random.normal(stream_key, dims, jnp.float32) * scale * level
    return jnp.minimum(jnp.maximum(values, -bound), bound).astype(kind)


def setup_inputs(seed: int = 0, part: int = 0) -> dict:
    key_list = jax.random.split(jax.random.key(seed), 5)
    part_splits = jax.random.split(jax.random.fold_in(key_list[4], part), 5)
    return {
        "tokens": draw_tokens(jax.random.fold_in(jax.random.fold_in(key_list[4], part), 71), part),
        "norm_gain": jnp.clip(1.0 + 0.18 * jax.random.normal(key_list[1], (D,), jnp.float32), 0.1, 1.9),
        "w_key": centred(key_list[2], (D, KVW), D ** -0.5, 0.0625, ((0, 4), (1, 4))),
        "w_value": centred(key_list[3], (D, KVW), D ** -0.5, 0.0625, ((0, 4), (1, 4))),
    }


rope_base = 500000.0

def rotate(projected, positions):
    row_count = projected.shape[0]
    head_count = projected.shape[1] // HEAD
    half_head = HEAD // 2
    frequency = rope_base ** (-2.0 * jnp.arange(half_head, dtype=jnp.float32) / HEAD)
    angles = positions.astype(jnp.float32)[:, None] * frequency[None, :]
    cosine = jnp.cos(angles)[:, None, :]
    sine = jnp.sin(angles)[:, None, :]
    split_heads = projected.reshape(row_count, head_count, HEAD)
    first = split_heads[:, :, :half_head]
    second = split_heads[:, :, half_head:]
    turned = jnp.concatenate([first * cosine - second * sine, second * cosine + first * sine], axis=2)
    return turned.reshape(row_count, head_count * HEAD)

def reference(tokens, norm_gain, w_key, w_value):
    widened = tokens.astype(jnp.float32)
    inverse_rms = lax.rsqrt(lax.optimization_barrier(jnp.mean(widened * widened, axis=1, keepdims=True)) + 1e-05)
    normed = (widened * inverse_rms * norm_gain.astype(jnp.float32)[None, :]).astype(jnp.bfloat16)
    weights = jnp.concatenate([w_key, w_value], axis=1)
    block = D // N_ROW

    def add_block(total, index):
        start = (index * block).astype(jnp.int32)
        rows = lax.dynamic_slice_in_dim(normed, start, block, 1)
        piece = lax.dynamic_slice_in_dim(weights, start, block, 0)
        partial_sum = jnp.dot(rows, piece, preferred_element_type=jnp.float32).astype(jnp.bfloat16)
        partial_sum = lax.optimization_barrier(partial_sum)
        return (total + partial_sum.astype(jnp.float32), None)
    start_total = jnp.zeros((LEN, 2 * KVW), jnp.float32)
    summed, unused = lax.scan(add_block, start_total, jnp.arange(N_ROW, dtype=jnp.int32))
    positions = jnp.arange(LEN, dtype=jnp.int32)
    key_rows = rotate(summed[:, :KVW], positions).astype(jnp.bfloat16)
    value_rows = summed[:, KVW:].astype(jnp.bfloat16)
    return (key_rows, value_rows)
```

```python
import jax
import jax.numpy as jnp
from jax import lax
from jax.sharding import PartitionSpec as P

HEAD = 128


rope_base = 500000.0


def rotate(projected, positions):
    row_count = projected.shape[0]
    head_count = projected.shape[1] // HEAD
    half_head = HEAD // 2
    frequency = rope_base ** (-2.0 * jnp.arange(half_head, dtype=jnp.float32) / HEAD)
    angles = positions.astype(jnp.float32)[:, None] * frequency[None, :]
    cosine = jnp.cos(angles)[:, None, :]
    sine = jnp.sin(angles)[:, None, :]
    split_heads = projected.reshape(row_count, head_count, HEAD)
    first = split_heads[:, :, :half_head]
    second = split_heads[:, :, half_head:]
    turned = jnp.concatenate(
        [first * cosine - second * sine, second * cosine + first * sine], axis=2
    )
    return turned.reshape(row_count, head_count * HEAD)


def body(tokens, norm_gain, w_key, w_value):
    dp_count = lax.axis_size("dp")
    row_count = lax.axis_size("row")
    col_count = lax.axis_size("col")
    dp_index = lax.axis_index("dp")
    row_index = lax.axis_index("row")
    col_index = lax.axis_index("col")
    own_rows, features = tokens.shape
    block, width = w_key.shape
    pair_count = 2 if dp_count % 2 == 0 else 1
    pair_index = dp_index % pair_count
    part = block // pair_count

    def swap(array, row_bits, pair_bits):
        pairs = []
        for d in range(dp_count):
            for r in range(row_count):
                target = (d ^ pair_bits) * row_count + (r ^ row_bits)
                pairs.append((d * row_count + r, target))
        return lax.ppermute(array, ("dp", "row"), pairs)

    def shift(array, step, sources):
        return lax.ppermute(array, "col", [(i, i + step) for i in sources])

    start = pair_index * part
    own_weights = jnp.concatenate(
        [
            lax.dynamic_slice_in_dim(w_key, start, part, 0),
            lax.dynamic_slice_in_dim(w_value, start, part, 0),
        ],
        axis=1,
    )
    groups = [[own_weights]]
    from_left, from_right = own_weights, own_weights
    for s in range(1, col_count):
        from_left = shift(from_left, 1, range(s - 1, col_count - 1))
        from_right = shift(from_right, -1, range(1, col_count - s + 1))
        if 2 * s < col_count:
            groups.append([from_left, from_right])
        else:
            groups.append([jnp.where(col_index >= s, from_left, from_right)])

    widened = tokens.astype(jnp.float32)
    inverse_rms = lax.rsqrt(jnp.mean(widened * widened, axis=1, keepdims=True) + 1e-05)
    normed = (widened * inverse_rms * norm_gain[None, :]).astype(jnp.bfloat16)
    order = [(r, d) for odd in (1, 0) for r in range(odd, row_count, 2) for d in range(pair_count)]
    half = len(order) // 2
    received = []
    for r, d in order:
        index = (row_index ^ r) * pair_count + (pair_index ^ d)
        piece = lax.dynamic_slice_in_dim(normed, index * part, part, 1)
        received.append(piece if (r, d) == (0, 0) else swap(piece, r, d))
    far = jnp.concatenate(received[:half], axis=0)
    near = jnp.concatenate(received[half:], axis=0)

    def reduce(weights):
        n = weights.shape[1]
        far_part = jnp.dot(far, weights, preferred_element_type=jnp.float32).astype(jnp.bfloat16)
        other = swap(far_part, 1, 0)
        near_part = jnp.dot(near, weights, preferred_element_type=jnp.float32)
        both = (near_part + other.astype(jnp.float32)).astype(jnp.bfloat16)
        both = both.reshape(half, own_rows, n)
        total = both[0].astype(jnp.float32)
        for k in range(1, half):
            r, d = order[half + k]
            total = total + swap(both[k], r, d).astype(jnp.float32)
        return total

    slots = []
    for group in groups:
        total = reduce(group[0] if len(group) == 1 else jnp.concatenate(group, axis=1))
        slots += [total[:, i * 2 * width : (i + 1) * 2 * width] for i in range(len(group))]
    stack = jnp.stack(slots)
    ordered = []
    for b in range(col_count):
        distance = jnp.abs(col_index - b)
        paired = (col_count - 1) // 2
        slot = jnp.where(
            distance == 0,
            0,
            jnp.where(
                distance <= paired,
                2 * distance - 1 + (b > col_index),
                distance + paired,
            ),
        )
        ordered.append(lax.dynamic_index_in_dim(stack, slot, 0, keepdims=False))
    key_sum = jnp.concatenate([o[:, :width] for o in ordered], axis=1)
    value_sum = jnp.concatenate([o[:, width:] for o in ordered], axis=1)
    positions = (row_index * col_count + col_index) * own_rows + jnp.arange(
        own_rows, dtype=jnp.int32
    )
    key_rows = rotate(key_sum, positions).astype(jnp.bfloat16)
    value_rows = value_sum.astype(jnp.bfloat16)
    return (key_rows, value_rows)


def solution(mesh):
    placed = (P(("dp", "row", "col"), None), P(), P("row", "col"), P("row", "col"))
    return jax.shard_map(
        body,
        mesh=mesh,
        in_specs=placed,
        out_specs=(P(("dp", "row", "col"), None), P(("dp", "row", "col"), None)),
        check_vma=False,
    )
```

```python
import functools

import jax
import jax.numpy as jnp
from jax import lax
from jax.experimental import pallas as pl
from jax.experimental.pallas import tpu as pltpu
from jax.sharding import PartitionSpec as P

HEAD = 128


rope_base = 500000.0


def rotation(positions):
    half_head = HEAD // 2
    frequency = rope_base ** (-2.0 * jnp.arange(half_head, dtype=jnp.float32) / HEAD)
    angles = positions.astype(jnp.float32)[:, None] * frequency[None, :]
    cosine = jnp.cos(angles)
    sine = jnp.sin(angles)
    return (
        jnp.concatenate([cosine, cosine], axis=1),
        jnp.concatenate([-sine, sine], axis=1),
    )


def params():
    return pltpu.CompilerParams(vmem_limit_bytes=24 * 1024 * 1024)


def norm_kernel(tokens_ref, gain_ref, out_ref, *, row_count, pair_count, part):
    widened = tokens_ref[...].astype(jnp.float32)
    mean = jnp.mean(widened * widened, axis=1, keepdims=True)
    normed = (widened * lax.rsqrt(mean + 1e-05) * gain_ref[...]).astype(jnp.bfloat16)
    for r in range(row_count):
        for d in range(pair_count):
            at = (r * pair_count + d) * part
            out_ref[d * row_count + r] = normed[:, at : at + part]


def normalise(tokens, norm_gain, row_count, pair_count, part):
    rows, features = tokens.shape
    step = 32
    count = row_count * pair_count
    return pl.pallas_call(
        functools.partial(
            norm_kernel, row_count=row_count, pair_count=pair_count, part=part
        ),
        grid=(rows // step,),
        in_specs=[
            pl.BlockSpec((step, features), lambda i: (i, 0)),
            pl.BlockSpec((1, features), lambda i: (0, 0)),
        ],
        out_specs=pl.BlockSpec((count, step, part), lambda i: (0, i, 0)),
        out_shape=jax.ShapeDtypeStruct((count, rows, part), jnp.bfloat16),
        compiler_params=params(),
        name="norm",
    )(tokens, norm_gain[None, :])


def split_kernel(place_ref, near_ref, far_ref, near_out, far_out):
    near_out[...] = near_ref[...]
    far_out[...] = far_ref[...]


def split(place, tile, pair_count, row_count):
    rows, part = tile.shape[1:]
    chips = row_count // 2 * pair_count

    def index(odd):
        def at(k, place):
            pair = place[0] ^ (k % pair_count)
            row = place[1] ^ ((k // pair_count) * 2 + odd)
            return (pair * row_count + row, 0, 0)

        return at

    block = (1, rows, part)
    out = pl.BlockSpec(block, lambda k, place: (k, 0, 0))
    near, far = pl.pallas_call(
        split_kernel,
        grid_spec=pltpu.PrefetchScalarGridSpec(
            num_scalar_prefetch=1,
            grid=(chips,),
            in_specs=[pl.BlockSpec(block, index(0)), pl.BlockSpec(block, index(1))],
            out_specs=[out, out],
        ),
        out_shape=[jax.ShapeDtypeStruct((chips, rows, part), jnp.bfloat16)] * 2,
        compiler_params=params(),
        name="split",
    )(place, tile, tile)
    return near.reshape(chips * rows, part), far.reshape(chips * rows, part)


def sum_kernel(place_ref, *refs, terms, kinds, width, outs):
    cosine_ref, sine_ref = refs[terms : terms + 2]
    out_refs = refs[-outs:]
    total = refs[0][0].astype(jnp.float32)
    for ref in refs[1:terms]:
        total = total + ref[...].astype(jnp.float32)
    for i, kind in enumerate(kinds):
        block = total[:, i * width : (i + 1) * width]
        out_ref = out_refs[i]
        if kind == "key":
            for h in range(width // HEAD):
                head = block[:, h * HEAD : (h + 1) * HEAD]
                turned = head * cosine_ref[...] + pltpu.roll(
                    head, HEAD // 2, 1
                ) * sine_ref[...]
                out_ref[:, h * HEAD : (h + 1) * HEAD] = turned.astype(jnp.bfloat16)
        else:
            out_ref[...] = block.astype(jnp.bfloat16)


def finish(place, both, others, tables, held, slots, kinds, width, columns):
    rows = both.shape[1]
    n = len(kinds) * width
    first_slot = slots[0]
    arrays = [both, *others, *tables]
    specs = [pl.BlockSpec((1, rows, n), lambda k, place: (0, 0, k))]
    specs += [pl.BlockSpec((rows, n), lambda k, place: (0, k)) for o in others]
    specs += [pl.BlockSpec((rows, HEAD), lambda k, place: (0, 0)) for t in tables]
    aliases = {}
    for i, h in enumerate(held):
        aliases[1 + len(arrays)] = i
        arrays.append(h)
        specs.append(pl.BlockSpec(memory_space=pl.ANY))
    out_spec = pl.BlockSpec(
        (rows, width), lambda k, place: (0, place[2] ^ (k + first_slot))
    )
    return pl.pallas_call(
        functools.partial(
            sum_kernel, terms=1 + len(others), kinds=kinds, width=width, outs=len(kinds)
        ),
        grid_spec=pltpu.PrefetchScalarGridSpec(
            num_scalar_prefetch=1,
            grid=(len(slots),),
            in_specs=specs,
            out_specs=[out_spec] * len(kinds),
        ),
        out_shape=[jax.ShapeDtypeStruct((rows, columns), jnp.bfloat16)] * len(kinds),
        input_output_aliases=aliases,
        compiler_params=params(),
        name="finish",
    )(place, *arrays)


def body(tokens, norm_gain, w_key, w_value):
    dp_count = lax.axis_size("dp")
    row_count = lax.axis_size("row")
    col_count = lax.axis_size("col")
    dp_index = lax.axis_index("dp")
    row_index = lax.axis_index("row")
    col_index = lax.axis_index("col")
    own_rows = tokens.shape[0]
    block, width = w_key.shape
    columns = width * col_count
    pair_count = 2 if dp_count % 2 == 0 else 1
    pair_index = dp_index % pair_count
    part = block // pair_count
    inner = ((col_index + 1) % 4) // 2
    place = jnp.stack([pair_index, row_index, col_index, inner]).astype(jnp.int32)

    def swap(array, row_bits, pair_bits):
        pairs = []
        for d in range(dp_count):
            for r in range(row_count):
                target = (d ^ pair_bits) * row_count + (r ^ row_bits)
                pairs.append((d * row_count + r, target))
        return lax.ppermute(array, ("dp", "row"), pairs)

    def exchange(array, bits, places=(0, 1, 2, 3)):
        return lax.ppermute(
            array, "col", [(i, i ^ bits) for i in range(col_count) if i % 4 in places]
        )

    positions = (row_index * col_count + col_index) * own_rows + jnp.arange(
        own_rows, dtype=jnp.int32
    )
    tables = rotation(positions)

    always = col_index < col_count

    def stage(work, *args):
        shapes = jax.eval_shape(work, *args)

        def skip(*args):
            return jax.tree.map(lambda s: jnp.zeros(s.shape, s.dtype), shapes)

        return lax.cond(always, work, skip, *args)

    start = pair_index * part
    own = jnp.concatenate(
        [lax.dynamic_slice_in_dim(w, start, part, 0) for w in (w_key, w_value)], axis=1
    )
    slot2 = exchange(own, 2)
    slot1 = exchange(own, 1)
    chips = [(r, d) for r in range(0, row_count, 2) for d in range(pair_count)]
    (tokens, own) = lax.optimization_barrier((tokens, own))
    def spread(tokens):
        parts = normalise(tokens, norm_gain, row_count, pair_count, part)
        groups = [
            [(g * pair_count + d) * row_count + r for d in range(pair_count) for r in range(row_count)]
            for g in range(dp_count // pair_count)
        ]
        return lax.all_to_all(
            parts,
            ("dp", "row"),
            split_axis=0,
            concat_axis=0,
            tiled=True,
            axis_index_groups=groups if len(groups) > 1 else None,
        )

    tile = stage(spread, tokens)

    def first(near, far, weights):
        shape = (len(chips), own_rows, -1)
        far_part = jnp.dot(far, weights, preferred_element_type=jnp.float32)
        other = swap(far_part.astype(jnp.bfloat16).reshape(shape), 1, 0)
        near_part = jnp.dot(near, weights, preferred_element_type=jnp.float32)
        both = near_part.reshape(shape) + other.astype(jnp.float32)
        return both.astype(jnp.bfloat16)

    def first_of(near, far, inner_weights, outer_weights):
        def dot(rows):
            def product(rows, weights):
                return jnp.dot(rows, weights, preferred_element_type=jnp.float32).astype(jnp.bfloat16)

            return lax.cond(
                inner == 1,
                lambda r, i, o: product(r, i),
                lambda r, i, o: product(r, o),
                rows,
                inner_weights,
                outer_weights,
            ).reshape(len(chips), own_rows, -1)

        other = swap(dot(far), 1, 0)
        return dot(near), other

    def second(both):
        return [swap(both[k], *chips[k]) for k in range(1, len(chips))]

    def add(both, held, slots, kinds, others=None):
        others = second(both) if others is None else others
        return finish(place, both, others, tables, held, slots, kinds, width, columns)

    kinds = ("key", "value")
    (tile, own) = lax.optimization_barrier((tile, own))
    def own_work(tile, own):
        near, far = split(place, tile, pair_count, row_count)
        return near, far, first(near, far, own)

    near, far, both0 = stage(own_work, tile, own)
    (near, far, both0, own, slot1, slot2) = lax.optimization_barrier((near, far, both0, own, slot1, slot2))
    outer = exchange(slot2, 1, (1, 2))
    middle = exchange(own, 3, (1, 2))

    def middle_work(near, far, both0, slot1, slot2):
        both12 = first(near, far, jnp.concatenate([slot1, slot2], axis=1))
        both = jnp.concatenate([both0, both12], axis=2)
        return add(both, [], (0, 1, 2), kinds)

    held = stage(middle_work, near, far, both0, slot1, slot2)
    (held, outer, middle) = lax.optimization_barrier((held, outer, middle))
    third = lax.optimization_barrier(jnp.where(inner == 1, middle, outer))
    held = add(first(near, far, third), held, (3,), kinds)
    blocks = [own, slot1, slot2, third]
    while len(blocks) < col_count:
        blocks += [exchange(w, len(blocks)) for w in blocks]
    for k in range(4, col_count):
        held = add(first(near, far, blocks[k]), held, (k,), kinds)
    key_rows, value_rows = held
    return (key_rows, value_rows)


def solution(mesh):
    placed = (P(("dp", "row", "col"), None), P(), P("row", "col"), P("row", "col"))
    return jax.shard_map(
        body,
        mesh=mesh,
        in_specs=placed,
        out_specs=(P(("dp", "row", "col"), None), P(("dp", "row", "col"), None)),
        check_vma=False,
    )
```

```python
import functools

import jax
import jax.numpy as jnp
from jax import lax
from jax.experimental import pallas as pl
from jax.experimental.pallas import tpu as pltpu
from jax.sharding import PartitionSpec as P

HEAD = 128


rope_base = 500000.0


def rotation(positions):
    half_head = HEAD // 2
    frequency = rope_base ** (-2.0 * jnp.arange(half_head, dtype=jnp.float32) / HEAD)
    angles = positions.astype(jnp.float32)[:, None] * frequency[None, :]
    cosine = jnp.cos(angles)
    sine = jnp.sin(angles)
    return (
        jnp.concatenate([cosine, cosine], axis=1),
        jnp.concatenate([-sine, sine], axis=1),
    )


def params():
    return pltpu.CompilerParams(vmem_limit_bytes=24 * 1024 * 1024)


def norm_kernel(tokens_ref, gain_ref, out_ref, *, row_count, pair_count, part):
    step = 32
    blocks = [(d * row_count + r, r * pair_count + d) for r in range(row_count) for d in range(pair_count)]
    count = len(blocks) * part

    @pl.loop(0, tokens_ref.shape[0], step=step)
    def _(at):
        rows = pl.ds(pl.multiple_of(at, step), step)

        def piece(k):
            return tokens_ref[rows, k * part : (k + 1) * part].astype(jnp.float32)

        squares = jnp.zeros((step, 128), jnp.float32)
        for _, k in blocks:
            square = piece(k) * piece(k)
            for j in range(0, part, 128):
                squares = squares + square[:, j : j + 128]
        mean = jnp.sum(squares, axis=1, keepdims=True) / count
        inverse_rms = lax.rsqrt(mean + 1e-05)
        for place, k in blocks:
            gain = gain_ref[:, k * part : (k + 1) * part]
            out_ref[place, rows, :] = (piece(k) * inverse_rms * gain).astype(jnp.bfloat16)


def normalise(tokens, norm_gain, row_count, pair_count, part):
    rows = tokens.shape[0]
    vmem = pl.BlockSpec(memory_space=pltpu.VMEM)
    return pl.pallas_call(
        functools.partial(
            norm_kernel, row_count=row_count, pair_count=pair_count, part=part
        ),
        in_specs=[vmem, vmem],
        out_specs=vmem,
        out_shape=pltpu.VMEM((row_count * pair_count, rows, part), jnp.bfloat16),
        compiler_params=params(),
        name="norm",
    )(tokens, norm_gain[None, :])


def own_kernel(place_ref, tile_ref, weights_ref, near_rows, far_rows, near_ref, far_ref, weights, sems, *, pair_count, row_count):
    rows = tile_ref.shape[1]
    copies = [pltpu.make_async_copy(weights_ref, weights, sems.at[2, 0])]
    halves = (near_rows, far_rows)
    for odd in (1, 0):
        for k in range(row_count // 2 * pair_count):
            pair = place_ref[0] ^ (k % pair_count)
            row = place_ref[1] ^ ((k // pair_count) * 2 + odd)
            copies.append(
                pltpu.make_async_copy(
                    tile_ref.at[pair * row_count + row],
                    halves[odd].at[pl.ds(k * rows, rows)],
                    sems.at[odd, k],
                )
            )
    for copy in copies:
        copy.start()
    for copy in copies:
        copy.wait()
    for half, out_ref in ((far_rows, far_ref), (near_rows, near_ref)):
        product = jnp.dot(half[...], weights[...], preferred_element_type=jnp.float32)
        out_ref[...] = product.reshape(out_ref.shape).astype(out_ref.dtype)


def project_own(place, tile, weights, pair_count, row_count):
    count, rows, part = tile.shape
    chips = count // 2
    n = weights.shape[1]
    vmem = pl.BlockSpec(memory_space=pltpu.VMEM)
    half = jax.ShapeDtypeStruct((chips * rows, part), jnp.bfloat16)
    return pl.pallas_call(
        functools.partial(own_kernel, pair_count=pair_count, row_count=row_count),
        in_specs=[pl.BlockSpec(memory_space=pltpu.SMEM)] + [pl.BlockSpec(memory_space=pl.ANY)] * 2,
        out_specs=[vmem] * 4,
        out_shape=[
            half,
            half,
            pltpu.VMEM((chips, rows, n), jnp.bfloat16),
            pltpu.VMEM((chips, rows, n), jnp.bfloat16),
        ],
        scratch_shapes=[
            pltpu.VMEM(weights.shape, jnp.bfloat16),
            pltpu.SemaphoreType.DMA((3, chips)),
        ],
        compiler_params=params(),
        name="project_own",
    )(place, tile, weights)


def sum_kernel(place_ref, *refs, terms, kinds, width, outs):
    cosine_ref, sine_ref = refs[terms : terms + 2]
    out_refs = refs[-outs:]
    total = refs[0][0].astype(jnp.float32)
    for ref in refs[1:terms]:
        total = total + ref[...].astype(jnp.float32)
    for i, kind in enumerate(kinds):
        block = total[:, i * width : (i + 1) * width]
        out_ref = out_refs[i]
        if kind == "key":
            for h in range(width // HEAD):
                head = block[:, h * HEAD : (h + 1) * HEAD]
                turned = head * cosine_ref[...] + pltpu.roll(
                    head, HEAD // 2, 1
                ) * sine_ref[...]
                out_ref[:, h * HEAD : (h + 1) * HEAD] = turned.astype(jnp.bfloat16)
        else:
            out_ref[...] = block.astype(jnp.bfloat16)


def finish(place, both, others, tables, held, slots, kinds, width, columns):
    rows = both.shape[1]
    n = len(kinds) * width
    first_slot = slots[0]
    arrays = [both, *others, *tables]
    specs = [pl.BlockSpec((1, rows, n), lambda k, place: (0, 0, k))]
    specs += [pl.BlockSpec((rows, n), lambda k, place: (0, k)) for o in others]
    specs += [pl.BlockSpec((rows, HEAD), lambda k, place: (0, 0)) for t in tables]
    aliases = {}
    for i, h in enumerate(held):
        aliases[1 + len(arrays)] = i
        arrays.append(h)
        specs.append(pl.BlockSpec(memory_space=pl.ANY))
    out_spec = pl.BlockSpec(
        (rows, width), lambda k, place: (0, place[2] ^ (k + first_slot))
    )
    return pl.pallas_call(
        functools.partial(
            sum_kernel, terms=1 + len(others), kinds=kinds, width=width, outs=len(kinds)
        ),
        grid_spec=pltpu.PrefetchScalarGridSpec(
            num_scalar_prefetch=1,
            grid=(len(slots),),
            in_specs=specs,
            out_specs=[out_spec] * len(kinds),
        ),
        out_shape=[jax.ShapeDtypeStruct((rows, columns), jnp.bfloat16)] * len(kinds),
        input_output_aliases=aliases,
        compiler_params=params(),
        name="finish",
    )(place, *arrays)


def body(tokens, norm_gain, w_key, w_value):
    dp_count = lax.axis_size("dp")
    row_count = lax.axis_size("row")
    col_count = lax.axis_size("col")
    dp_index = lax.axis_index("dp")
    row_index = lax.axis_index("row")
    col_index = lax.axis_index("col")
    own_rows = tokens.shape[0]
    block, width = w_key.shape
    columns = width * col_count
    pair_count = 2 if dp_count % 2 == 0 else 1
    pair_index = dp_index % pair_count
    part = block // pair_count
    inner = ((col_index + 1) % 4) // 2
    place = jnp.stack([pair_index, row_index, col_index, inner]).astype(jnp.int32)

    def swap(array, row_bits, pair_bits):
        pairs = []
        for d in range(dp_count):
            for r in range(row_count):
                target = (d ^ pair_bits) * row_count + (r ^ row_bits)
                pairs.append((d * row_count + r, target))
        return lax.ppermute(array, ("dp", "row"), pairs)

    def exchange(array, bits, places=(0, 1, 2, 3)):
        return lax.ppermute(
            array, "col", [(i, i ^ bits) for i in range(col_count) if i % 4 in places]
        )

    positions = (row_index * col_count + col_index) * own_rows + jnp.arange(
        own_rows, dtype=jnp.int32
    )
    tables = rotation(positions)

    always = col_index < col_count

    def stage(work, *args):
        shapes = jax.eval_shape(work, *args)

        def skip(*args):
            return jax.tree.map(lambda s: jnp.zeros(s.shape, s.dtype), shapes)

        return lax.cond(always, work, skip, *args)

    start = pair_index * part
    own = jnp.concatenate(
        [lax.dynamic_slice_in_dim(w, start, part, 0) for w in (w_key, w_value)], axis=1
    )
    slot2 = exchange(own, 2)
    slot1 = exchange(own, 1)
    chips = [(r, d) for r in range(0, row_count, 2) for d in range(pair_count)]
    (tokens, own) = lax.optimization_barrier((tokens, own))
    parts = normalise(tokens, norm_gain, row_count, pair_count, part)

    def spread(parts):
        groups = [
            [(g * pair_count + d) * row_count + r for d in range(pair_count) for r in range(row_count)]
            for g in range(dp_count // pair_count)
        ]
        return lax.all_to_all(
            parts,
            ("dp", "row"),
            split_axis=0,
            concat_axis=0,
            tiled=True,
            axis_index_groups=groups if len(groups) > 1 else None,
        )

    tile = stage(spread, parts)

    shape = (len(chips), own_rows, -1)

    def dot(rows, weights):
        product = jnp.dot(rows, weights, preferred_element_type=jnp.float32)
        return product.reshape(shape)

    def far_parts(blocks):
        return [dot(far, w).astype(jnp.bfloat16) for w in blocks]

    def first(near, far_parts, blocks):
        others = [swap(part, 1, 0) for part in far_parts]
        return [
            (dot(near, w) + other.astype(jnp.float32)).astype(jnp.bfloat16)
            for w, other in zip(blocks, others)
        ]

    def second(both):
        return [swap(both[k], *chips[k]) for k in range(1, len(chips))]

    def add(both, held, slots, kinds, others=None):
        others = second(both) if others is None else others
        return finish(place, both, others, tables, held, slots, kinds, width, columns)

    kinds = ("key", "value")
    def both_cores(near_part, far_part):
        other = swap(far_part, 1, 0)
        return (near_part.astype(jnp.float32) + other.astype(jnp.float32)).astype(jnp.bfloat16)

    (tile, own) = lax.optimization_barrier((tile, own))
    near, far, near0, far0 = project_own(place, tile, own, pair_count, row_count)
    held = stage(lambda n, f: add(both_cores(n, f), [], (0,), kinds), near0, far0)
    (near, far, held, own, slot2) = lax.optimization_barrier((near, far, held, own, slot2))
    outer = exchange(slot2, 1)
    middle = exchange(own, 3, (1, 2))

    def middle_work(near, far12, held, slot1, slot2):
        both12 = first(near, far12, [slot1, slot2])
        return add(jnp.concatenate(both12, axis=2), held, (1, 2), kinds)

    held = stage(middle_work, near, far_parts([slot1, slot2]), held, slot1, slot2)
    (held, outer, middle) = lax.optimization_barrier((held, outer, middle))
    third = lax.optimization_barrier(jnp.where(inner == 1, middle, outer))
    held = add(first(near, far_parts([third]), [third])[0], held, (3,), kinds)
    blocks = [own, slot1, slot2, third]
    while len(blocks) < col_count:
        blocks += [exchange(w, len(blocks)) for w in blocks]
    for k in range(4, col_count):
        held = add(first(near, far_parts([blocks[k]]), [blocks[k]])[0], held, (k,), kinds)
    key_rows, value_rows = held
    return (key_rows, value_rows)


def solution(mesh):
    placed = (P(("dp", "row", "col"), None), P(), P("row", "col"), P("row", "col"))
    return jax.shard_map(
        body,
        mesh=mesh,
        in_specs=placed,
        out_specs=(P(("dp", "row", "col"), None), P(("dp", "row", "col"), None)),
        check_vma=False,
    )
```

```python
import functools

import jax
import jax.numpy as jnp
from jax import lax
from jax.experimental import pallas as pl
from jax.experimental.pallas import tpu as pltpu
from jax.sharding import PartitionSpec as P

HEAD = 128


rope_base = 500000.0


def rotation(positions):
    half_head = HEAD // 2
    frequency = rope_base ** (-2.0 * jnp.arange(half_head, dtype=jnp.float32) / HEAD)
    angles = positions.astype(jnp.float32)[:, None] * frequency[None, :]
    cosine = jnp.cos(angles)
    sine = jnp.sin(angles)
    return (
        jnp.concatenate([cosine, cosine], axis=1),
        jnp.concatenate([-sine, sine], axis=1),
    )


def params():
    return pltpu.CompilerParams(vmem_limit_bytes=24 * 1024 * 1024)


def norm_kernel(tokens_ref, gain_ref, out_ref, *, row_count, pair_count, part):
    step = 32
    blocks = [(d * row_count + r, r * pair_count + d) for r in range(row_count) for d in range(pair_count)]
    count = len(blocks) * part

    @pl.loop(0, tokens_ref.shape[0], step=step)
    def _(at):
        rows = pl.ds(pl.multiple_of(at, step), step)

        def piece(k):
            return tokens_ref[rows, k * part : (k + 1) * part].astype(jnp.float32)

        squares = jnp.zeros((step, 128), jnp.float32)
        for _, k in blocks:
            square = piece(k) * piece(k)
            for j in range(0, part, 128):
                squares = squares + square[:, j : j + 128]
        mean = jnp.sum(squares, axis=1, keepdims=True) / count
        inverse_rms = lax.rsqrt(mean + 1e-05)
        for place, k in blocks:
            gain = gain_ref[:, k * part : (k + 1) * part]
            out_ref[place, rows, :] = (piece(k) * inverse_rms * gain).astype(jnp.bfloat16)


def normalise(tokens, norm_gain, row_count, pair_count, part):
    rows = tokens.shape[0]
    vmem = pl.BlockSpec(memory_space=pltpu.VMEM)
    return pl.pallas_call(
        functools.partial(
            norm_kernel, row_count=row_count, pair_count=pair_count, part=part
        ),
        in_specs=[vmem, vmem],
        out_specs=vmem,
        out_shape=pltpu.VMEM((row_count * pair_count, rows, part), jnp.bfloat16),
        compiler_params=params(),
        name="norm",
    )(tokens, norm_gain[None, :])


def own_kernel(place_ref, tile_ref, weights_ref, near_rows, far_rows, near_ref, far_ref, weights, sems, *, pair_count, row_count):
    rows = tile_ref.shape[1]
    copies = [pltpu.make_async_copy(weights_ref, weights, sems.at[2, 0])]
    halves = (near_rows, far_rows)
    for odd in (1, 0):
        for k in range(row_count // 2 * pair_count):
            pair = place_ref[0] ^ (k % pair_count)
            row = place_ref[1] ^ ((k // pair_count) * 2 + odd)
            copies.append(
                pltpu.make_async_copy(
                    tile_ref.at[pair * row_count + row],
                    halves[odd].at[pl.ds(k * rows, rows)],
                    sems.at[odd, k],
                )
            )
    for copy in copies:
        copy.start()
    for copy in copies:
        copy.wait()
    for half, out_ref in ((far_rows, far_ref), (near_rows, near_ref)):
        product = jnp.dot(half[...], weights[...], preferred_element_type=jnp.float32)
        out_ref[...] = product.reshape(out_ref.shape).astype(out_ref.dtype)


def project_own(place, tile, weights, pair_count, row_count):
    count, rows, part = tile.shape
    chips = count // 2
    n = weights.shape[1]
    vmem = pl.BlockSpec(memory_space=pltpu.VMEM)
    half = pltpu.HBM((chips * rows, part), jnp.bfloat16)
    return pl.pallas_call(
        functools.partial(own_kernel, pair_count=pair_count, row_count=row_count),
        in_specs=[pl.BlockSpec(memory_space=pltpu.SMEM)] + [pl.BlockSpec(memory_space=pl.ANY)] * 2,
        out_specs=[vmem] * 4,
        out_shape=[
            half,
            half,
            pltpu.VMEM((chips, rows, n), jnp.bfloat16),
            pltpu.VMEM((chips, rows, n), jnp.bfloat16),
        ],
        scratch_shapes=[
            pltpu.VMEM(weights.shape, jnp.bfloat16),
            pltpu.SemaphoreType.DMA((3, chips)),
        ],
        compiler_params=params(),
        name="project_own",
    )(place, tile, weights)


def pair_kernel(near_hbm, far_hbm, *refs, count):
    blocks, (near_ref, far_ref) = refs[:count], refs[count : count + 2]
    near, far, weights, sems = refs[count + 2 :]
    n = weights.shape[2]
    copies = [pltpu.make_async_copy(far_hbm, far, sems.at[0])]
    copies += [
        pltpu.make_async_copy(block, weights.at[i], sems.at[2 + i])
        for i, block in enumerate(blocks)
    ]
    copies.append(pltpu.make_async_copy(near_hbm, near, sems.at[1]))
    for copy in copies:
        copy.start()

    def write(rows, out_ref, i):
        product = jnp.dot(rows[...], weights[i], preferred_element_type=jnp.float32)
        shape = out_ref.shape[:2] + (n,)
        out_ref[:, :, i * n : (i + 1) * n] = product.reshape(shape).astype(out_ref.dtype)

    copies[0].wait()
    for i in range(count):
        copies[1 + i].wait()
        write(far, far_ref, i)
    copies[-1].wait()
    for i in range(count):
        write(near, near_ref, i)


def project_both(near, far, blocks, rows):
    part, n = blocks[0].shape
    count = len(blocks)
    chips = near.shape[0] // rows
    vmem = pl.BlockSpec(memory_space=pltpu.VMEM)
    out = pltpu.VMEM((chips, rows, n * count), jnp.bfloat16)
    return pl.pallas_call(
        functools.partial(pair_kernel, count=count),
        in_specs=[pl.BlockSpec(memory_space=pl.ANY)] * (2 + count),
        out_specs=[vmem, vmem],
        out_shape=[out, out],
        scratch_shapes=[
            pltpu.VMEM(near.shape, jnp.bfloat16),
            pltpu.VMEM(far.shape, jnp.bfloat16),
            pltpu.VMEM((count, part, n), jnp.bfloat16),
            pltpu.SemaphoreType.DMA((2 + count,)),
        ],
        compiler_params=pltpu.CompilerParams(vmem_limit_bytes=24 * 1024 * 1024),
        name="project_both",
    )(near, far, *blocks)


def sum_kernel(place_ref, *refs, terms, slots, kinds, width, held):
    cosine_ref, sine_ref = refs[terms : terms + 2]
    first_out = terms + 2 + held
    out_refs = refs[first_out : first_out + len(kinds)]
    blocks_ref, sems = refs[first_out + len(kinds) :]
    copies = []
    for s, slot in enumerate(slots):
        for i, kind in enumerate(kinds):
            at = (s * len(kinds) + i) * width
            block = refs[0][0, :, at : at + width].astype(jnp.float32)
            for ref in refs[1:terms]:
                block = block + ref[:, at : at + width].astype(jnp.float32)
            if kind == "key":
                turned = []
                for h in range(0, width, HEAD):
                    head = block[:, h : h + HEAD]
                    other = pltpu.roll(head, HEAD // 2, 1)
                    turned.append(head * cosine_ref[...] + other * sine_ref[...])
                block = jnp.concatenate(turned, axis=1)
            blocks_ref[s, i] = block.astype(jnp.bfloat16)
            column = pl.multiple_of((place_ref[2] ^ slot) * width, width)
            copy = pltpu.make_async_copy(
                blocks_ref.at[s, i], out_refs[i].at[:, pl.ds(column, width)], sems.at[s, i]
            )
            copy.start()
            copies.append(copy)
    for copy in copies:
        copy.wait()


def finish(place, both, others, tables, held, slots, kinds, width, columns):
    rows = both.shape[1]
    arrays = [both, *others, *tables]
    vmem = pl.BlockSpec(memory_space=pltpu.VMEM)
    specs = [pl.BlockSpec(memory_space=pltpu.SMEM)] + [vmem] * len(arrays)
    specs += [pl.BlockSpec(memory_space=pl.ANY)] * len(held)
    return pl.pallas_call(
        functools.partial(
            sum_kernel,
            terms=1 + len(others),
            slots=slots,
            kinds=kinds,
            width=width,
            held=len(held),
        ),
        in_specs=specs,
        out_specs=[pl.BlockSpec(memory_space=pl.ANY)] * len(kinds),
        out_shape=[jax.ShapeDtypeStruct((rows, columns), jnp.bfloat16)] * len(kinds),
        scratch_shapes=[
            pltpu.VMEM((len(slots), len(kinds), rows, width), jnp.bfloat16),
            pltpu.SemaphoreType.DMA((len(slots), len(kinds))),
        ],
        input_output_aliases={1 + len(arrays) + i: i for i in range(len(held))},
        compiler_params=params(),
        name="finish",
    )(place, *arrays, *held)


def body(tokens, norm_gain, w_key, w_value):
    dp_count = lax.axis_size("dp")
    row_count = lax.axis_size("row")
    col_count = lax.axis_size("col")
    dp_index = lax.axis_index("dp")
    row_index = lax.axis_index("row")
    col_index = lax.axis_index("col")
    own_rows = tokens.shape[0]
    block, width = w_key.shape
    columns = width * col_count
    pair_count = 2 if dp_count % 2 == 0 else 1
    pair_index = dp_index % pair_count
    part = block // pair_count
    inner = ((col_index + 1) % 4) // 2
    place = jnp.stack([pair_index, row_index, col_index, inner]).astype(jnp.int32)

    def swap(array, row_bits, pair_bits):
        pairs = []
        for d in range(dp_count):
            for r in range(row_count):
                target = (d ^ pair_bits) * row_count + (r ^ row_bits)
                pairs.append((d * row_count + r, target))
        return lax.ppermute(array, ("dp", "row"), pairs)

    def exchange(array, bits, places=(0, 1, 2, 3)):
        return lax.ppermute(
            array, "col", [(i, i ^ bits) for i in range(col_count) if i % 4 in places]
        )

    positions = (row_index * col_count + col_index) * own_rows + jnp.arange(
        own_rows, dtype=jnp.int32
    )
    tables = rotation(positions)

    always = col_index < col_count

    def stage(work, *args):
        shapes = jax.eval_shape(work, *args)

        def skip(*args):
            return jax.tree.map(lambda s: jnp.zeros(s.shape, s.dtype), shapes)

        return lax.cond(always, work, skip, *args)

    start = pair_index * part
    own = jnp.concatenate(
        [lax.dynamic_slice_in_dim(w, start, part, 0) for w in (w_key, w_value)], axis=1
    )
    slot2 = exchange(own, 2)
    slot1 = exchange(own, 1)
    chips = [(r, d) for r in range(0, row_count, 2) for d in range(pair_count)]
    (tokens, own) = lax.optimization_barrier((tokens, own))
    parts = normalise(tokens, norm_gain, row_count, pair_count, part)

    def spread(parts):
        groups = [
            [(g * pair_count + d) * row_count + r for d in range(pair_count) for r in range(row_count)]
            for g in range(dp_count // pair_count)
        ]
        return lax.all_to_all(
            parts,
            ("dp", "row"),
            split_axis=0,
            concat_axis=0,
            tiled=True,
            axis_index_groups=groups if len(groups) > 1 else None,
        )

    tile = stage(spread, parts)

    shape = (len(chips), own_rows, -1)

    def dot(rows, weights):
        product = jnp.dot(rows, weights, preferred_element_type=jnp.float32)
        return product.reshape(shape)

    def far_parts(blocks):
        return [dot(far, w).astype(jnp.bfloat16) for w in blocks]

    def first(near, far_parts, blocks):
        others = [swap(part, 1, 0) for part in far_parts]
        return [
            (dot(near, w) + other.astype(jnp.float32)).astype(jnp.bfloat16)
            for w, other in zip(blocks, others)
        ]

    def second(both):
        return [swap(both[k], *chips[k]) for k in range(1, len(chips))]

    def add(both, held, slots, kinds, others=None):
        others = second(both) if others is None else others
        return finish(place, both, others, tables, held, slots, kinds, width, columns)

    kinds = ("key", "value")
    def both_cores(near_part, far_part):
        other = swap(far_part, 1, 0)
        return (near_part.astype(jnp.float32) + other.astype(jnp.float32)).astype(jnp.bfloat16)

    (tile, own) = lax.optimization_barrier((tile, own))
    near, far, near0, far0 = project_own(place, tile, own, pair_count, row_count)

    def sums(near_part, far_part):
        both = both_cores(near_part, far_part)
        return both[:1], second(both)

    sums0 = stage(sums, near0, far0)
    (near, far, sums0, own, slot2) = lax.optimization_barrier((near, far, sums0, own, slot2))
    outer = exchange(slot2, 1)
    middle = exchange(own, 3, (1, 2))
    near12, far12 = project_both(near, far, [slot1, slot2], own_rows)
    sums12 = stage(sums, near12, far12)
    (sums0, sums12, outer, middle) = lax.optimization_barrier((sums0, sums12, outer, middle))
    third = lax.optimization_barrier(jnp.where(inner == 1, middle, outer))
    both3 = first(near, far_parts([third]), [third])[0]
    others3 = second(both3)
    held = add(sums0[0], [], (0,), kinds, sums0[1])
    held = add(sums12[0], held, (1, 2), kinds, sums12[1])
    held = add(both3, held, (3,), kinds, others3)
    blocks = [own, slot1, slot2, third]
    while len(blocks) < col_count:
        blocks += [exchange(w, len(blocks)) for w in blocks]
    for k in range(4, col_count):
        held = add(first(near, far_parts([blocks[k]]), [blocks[k]])[0], held, (k,), kinds)
    key_rows, value_rows = held
    return (key_rows, value_rows)


def solution(mesh):
    placed = (P(("dp", "row", "col"), None), P(), P("row", "col"), P("row", "col"))
    return jax.shard_map(
        body,
        mesh=mesh,
        in_specs=placed,
        out_specs=(P(("dp", "row", "col"), None), P(("dp", "row", "col"), None)),
        check_vma=False,
    )
```

```python
import functools

import jax
import jax.numpy as jnp
from jax import lax
from jax.experimental import pallas as pl
from jax.experimental.pallas import tpu as pltpu
from jax.sharding import PartitionSpec as P

HEAD = 128


rope_base = 500000.0


def rotation(positions):
    half_head = HEAD // 2
    frequency = rope_base ** (-2.0 * jnp.arange(half_head, dtype=jnp.float32) / HEAD)
    angles = positions.astype(jnp.float32)[:, None] * frequency[None, :]
    cosine = jnp.cos(angles)
    sine = jnp.sin(angles)
    return (
        jnp.concatenate([cosine, cosine], axis=1),
        jnp.concatenate([-sine, sine], axis=1),
    )


def params():
    return pltpu.CompilerParams(vmem_limit_bytes=24 * 1024 * 1024)


def norm_kernel(tokens_hbm, gain_hbm, out_ref, tokens, gain, sems, *, row_count, pair_count, part):
    step = sems_step(tokens_hbm.shape[0])
    blocks = [
        (d * row_count + r, r * pair_count + d)
        for r in range(row_count)
        for d in range(pair_count)
    ]
    copies = [pltpu.make_async_copy(gain_hbm, gain, sems.at[0])]
    for i in range(tokens_hbm.shape[0] // step):
        rows = pl.ds(i * step, step)
        copies.append(
            pltpu.make_async_copy(tokens_hbm.at[rows], tokens.at[rows], sems.at[1 + i])
        )
    for copy in copies:
        copy.start()
    copies[0].wait()
    for i, copy in enumerate(copies[1:]):
        copy.wait()
        rows = pl.ds(i * step, step)

        def piece(k):
            return tokens[rows, k * part : (k + 1) * part].astype(jnp.float32)

        squares = jnp.zeros((step, 128), jnp.float32)
        for _, k in blocks:
            square = piece(k) * piece(k)
            for j in range(0, part, 128):
                squares = squares + square[:, j : j + 128]
        mean = jnp.sum(squares, axis=1, keepdims=True) / (len(blocks) * part)
        inverse_rms = lax.rsqrt(mean + 1e-05)
        for place, k in blocks:
            scaled = piece(k) * inverse_rms * gain[:, k * part : (k + 1) * part]
            out_ref[place, rows, :] = scaled.astype(jnp.bfloat16)


def sems_step(rows):
    return min(32, rows)


def normalise(tokens, norm_gain, row_count, pair_count, part):
    rows, features = tokens.shape
    anywhere = pl.BlockSpec(memory_space=pl.ANY)
    return pl.pallas_call(
        functools.partial(
            norm_kernel, row_count=row_count, pair_count=pair_count, part=part
        ),
        in_specs=[anywhere, anywhere],
        out_specs=pl.BlockSpec(memory_space=pltpu.VMEM),
        out_shape=pltpu.VMEM((row_count * pair_count, rows, part), jnp.bfloat16),
        scratch_shapes=[
            pltpu.VMEM((rows, features), jnp.bfloat16),
            pltpu.VMEM((1, features), jnp.float32),
            pltpu.SemaphoreType.DMA((1 + rows // sems_step(rows),)),
        ],
        compiler_params=params(),
        name="norm",
    )(tokens, norm_gain[None, :])


def own_kernel(place_ref, tile_ref, weights_ref, near_rows, far_rows, near_ref, far_ref, weights, sems, *, pair_count, row_count):
    rows = tile_ref.shape[1]
    copies = [pltpu.make_async_copy(weights_ref, weights, sems.at[2, 0])]
    halves = (near_rows, far_rows)
    for odd in (1, 0):
        for k in range(row_count // 2 * pair_count):
            pair = place_ref[0] ^ (k % pair_count)
            row = place_ref[1] ^ ((k // pair_count) * 2 + odd)
            copies.append(
                pltpu.make_async_copy(
                    tile_ref.at[pair * row_count + row],
                    halves[odd].at[pl.ds(k * rows, rows)],
                    sems.at[odd, k],
                )
            )
    for copy in copies:
        copy.start()
    for copy in copies:
        copy.wait()
    for half, out_ref in ((far_rows, far_ref), (near_rows, near_ref)):
        product = jnp.dot(half[...], weights[...], preferred_element_type=jnp.float32)
        out_ref[...] = product.reshape(out_ref.shape).astype(out_ref.dtype)


def project_own(place, tile, weights, pair_count, row_count):
    count, rows, part = tile.shape
    chips = count // 2
    n = weights.shape[1]
    vmem = pl.BlockSpec(memory_space=pltpu.VMEM)
    half = pltpu.HBM((chips * rows, part), jnp.bfloat16)
    return pl.pallas_call(
        functools.partial(own_kernel, pair_count=pair_count, row_count=row_count),
        in_specs=[pl.BlockSpec(memory_space=pltpu.SMEM)] + [pl.BlockSpec(memory_space=pl.ANY)] * 2,
        out_specs=[vmem] * 4,
        out_shape=[
            half,
            half,
            pltpu.VMEM((chips, rows, n), jnp.bfloat16),
            pltpu.VMEM((chips, rows, n), jnp.bfloat16),
        ],
        scratch_shapes=[
            pltpu.VMEM(weights.shape, jnp.bfloat16),
            pltpu.SemaphoreType.DMA((3, chips)),
        ],
        compiler_params=params(),
        name="project_own",
    )(place, tile, weights)


def pair_kernel(near_hbm, far_hbm, *refs, count):
    blocks, (near_ref, far_ref) = refs[:count], refs[count : count + 2]
    near, far, weights, sems = refs[count + 2 :]
    n = weights.shape[2]
    copies = [pltpu.make_async_copy(far_hbm, far, sems.at[0])]
    copies += [
        pltpu.make_async_copy(block, weights.at[i], sems.at[2 + i])
        for i, block in enumerate(blocks)
    ]
    copies.append(pltpu.make_async_copy(near_hbm, near, sems.at[1]))
    for copy in copies:
        copy.start()

    def write(rows, out_ref, i):
        product = jnp.dot(rows[...], weights[i], preferred_element_type=jnp.float32)
        shape = out_ref.shape[:2] + (n,)
        out_ref[:, :, i * n : (i + 1) * n] = product.reshape(shape).astype(out_ref.dtype)

    copies[0].wait()
    for i in range(count):
        copies[1 + i].wait()
        write(far, far_ref, i)
    copies[-1].wait()
    for i in range(count):
        write(near, near_ref, i)


def project_both(near, far, blocks, rows):
    part, n = blocks[0].shape
    count = len(blocks)
    chips = near.shape[0] // rows
    vmem = pl.BlockSpec(memory_space=pltpu.VMEM)
    out = pltpu.VMEM((chips, rows, n * count), jnp.bfloat16)
    return pl.pallas_call(
        functools.partial(pair_kernel, count=count),
        in_specs=[pl.BlockSpec(memory_space=pl.ANY)] * (2 + count),
        out_specs=[vmem, vmem],
        out_shape=[out, out],
        scratch_shapes=[
            pltpu.VMEM(near.shape, jnp.bfloat16),
            pltpu.VMEM(far.shape, jnp.bfloat16),
            pltpu.VMEM((count, part, n), jnp.bfloat16),
            pltpu.SemaphoreType.DMA((2 + count,)),
        ],
        compiler_params=pltpu.CompilerParams(vmem_limit_bytes=58 * 1024 * 1024),
        name="project_both",
    )(near, far, *blocks)


def sum_kernel(place_ref, *refs, terms, slots, kinds, width, held):
    cosine_ref, sine_ref = refs[terms : terms + 2]
    first_out = terms + 2 + held
    out_refs = refs[first_out : first_out + len(kinds)]
    blocks_ref, sems = refs[first_out + len(kinds) :]
    copies = []
    for s, slot in enumerate(slots):
        for i, kind in enumerate(kinds):
            at = (s * len(kinds) + i) * width
            block = refs[0][0, :, at : at + width].astype(jnp.float32)
            for ref in refs[1:terms]:
                block = block + ref[:, at : at + width].astype(jnp.float32)
            if kind == "key":
                turned = []
                for h in range(0, width, HEAD):
                    head = block[:, h : h + HEAD]
                    other = pltpu.roll(head, HEAD // 2, 1)
                    turned.append(head * cosine_ref[...] + other * sine_ref[...])
                block = jnp.concatenate(turned, axis=1)
            blocks_ref[s, i] = block.astype(jnp.bfloat16)
            column = pl.multiple_of((place_ref[2] ^ slot) * width, width)
            copy = pltpu.make_async_copy(
                blocks_ref.at[s, i], out_refs[i].at[:, pl.ds(column, width)], sems.at[s, i]
            )
            copy.start()
            copies.append(copy)
    for copy in copies:
        copy.wait()


def finish(place, both, others, tables, held, slots, kinds, width, columns):
    rows = both.shape[1]
    arrays = [both, *others, *tables]
    vmem = pl.BlockSpec(memory_space=pltpu.VMEM)
    specs = [pl.BlockSpec(memory_space=pltpu.SMEM)] + [vmem] * len(arrays)
    specs += [pl.BlockSpec(memory_space=pl.ANY)] * len(held)
    return pl.pallas_call(
        functools.partial(
            sum_kernel,
            terms=1 + len(others),
            slots=slots,
            kinds=kinds,
            width=width,
            held=len(held),
        ),
        in_specs=specs,
        out_specs=[pl.BlockSpec(memory_space=pl.ANY)] * len(kinds),
        out_shape=[jax.ShapeDtypeStruct((rows, columns), jnp.bfloat16)] * len(kinds),
        scratch_shapes=[
            pltpu.VMEM((len(slots), len(kinds), rows, width), jnp.bfloat16),
            pltpu.SemaphoreType.DMA((len(slots), len(kinds))),
        ],
        input_output_aliases={1 + len(arrays) + i: i for i in range(len(held))},
        compiler_params=params(),
        name="finish",
    )(place, *arrays, *held)


def body(tokens, norm_gain, w_key, w_value):
    dp_count = lax.axis_size("dp")
    row_count = lax.axis_size("row")
    col_count = lax.axis_size("col")
    dp_index = lax.axis_index("dp")
    row_index = lax.axis_index("row")
    col_index = lax.axis_index("col")
    own_rows = tokens.shape[0]
    block, width = w_key.shape
    columns = width * col_count
    pair_count = 2 if dp_count % 2 == 0 else 1
    pair_index = dp_index % pair_count
    part = block // pair_count
    inner = ((col_index + 1) % 4) // 2
    place = jnp.stack([pair_index, row_index, col_index, inner]).astype(jnp.int32)

    def swap(array, row_bits, pair_bits):
        pairs = []
        for d in range(dp_count):
            for r in range(row_count):
                target = (d ^ pair_bits) * row_count + (r ^ row_bits)
                pairs.append((d * row_count + r, target))
        return lax.ppermute(array, ("dp", "row"), pairs)

    def exchange(array, bits, places=(0, 1, 2, 3)):
        return lax.ppermute(
            array, "col", [(i, i ^ bits) for i in range(col_count) if i % 4 in places]
        )

    positions = (row_index * col_count + col_index) * own_rows + jnp.arange(
        own_rows, dtype=jnp.int32
    )
    tables = rotation(positions)

    always = col_index < col_count

    def stage(work, *args):
        shapes = jax.eval_shape(work, *args)

        def skip(*args):
            return jax.tree.map(lambda s: jnp.zeros(s.shape, s.dtype), shapes)

        return lax.cond(always, work, skip, *args)

    start = pair_index * part
    own = jnp.concatenate(
        [lax.dynamic_slice_in_dim(w, start, part, 0) for w in (w_key, w_value)], axis=1
    )
    slot2 = exchange(own, 2)
    slot1 = exchange(own, 1)
    chips = [(r, d) for r in range(0, row_count, 2) for d in range(pair_count)]
    (tokens, own) = lax.optimization_barrier((tokens, own))
    def spread(tokens):
        parts = normalise(tokens, norm_gain, row_count, pair_count, part)
        groups = [
            [(g * pair_count + d) * row_count + r for d in range(pair_count) for r in range(row_count)]
            for g in range(dp_count // pair_count)
        ]
        return lax.all_to_all(
            parts,
            ("dp", "row"),
            split_axis=0,
            concat_axis=0,
            tiled=True,
            axis_index_groups=groups if len(groups) > 1 else None,
        )

    tile = stage(spread, tokens)

    shape = (len(chips), own_rows, -1)

    def dot(rows, weights):
        product = jnp.dot(rows, weights, preferred_element_type=jnp.float32)
        return product.reshape(shape)

    def far_parts(blocks):
        return [dot(far, w).astype(jnp.bfloat16) for w in blocks]

    def first(near, far_parts, blocks):
        others = [swap(part, 1, 0) for part in far_parts]
        return [
            (dot(near, w) + other.astype(jnp.float32)).astype(jnp.bfloat16)
            for w, other in zip(blocks, others)
        ]

    def second(both):
        return [swap(both[k], *chips[k]) for k in range(1, len(chips))]

    def add(both, held, slots, kinds, others=None):
        others = second(both) if others is None else others
        return finish(place, both, others, tables, held, slots, kinds, width, columns)

    kinds = ("key", "value")
    def both_cores(near_part, far_part):
        other = swap(far_part, 1, 0)
        return (near_part.astype(jnp.float32) + other.astype(jnp.float32)).astype(jnp.bfloat16)

    (tile, own) = lax.optimization_barrier((tile, own))
    near, far, near0, far0 = project_own(place, tile, own, pair_count, row_count)

    def sums(near_part, far_part):
        both = both_cores(near_part, far_part)
        return both[:1], second(both)

    sums0 = stage(sums, near0, far0)
    (near, far, sums0, own, slot2) = lax.optimization_barrier((near, far, sums0, own, slot2))
    outer = exchange(slot2, 1)
    middle = exchange(own, 3, (1, 2))
    near12, far12 = project_both(near, far, [slot1, slot2], own_rows)
    sums12 = stage(sums, near12, far12)
    (sums0, sums12, outer, middle) = lax.optimization_barrier((sums0, sums12, outer, middle))
    third = lax.optimization_barrier(jnp.where(inner == 1, middle, outer))
    both3 = first(near, far_parts([third]), [third])[0]
    others3 = second(both3)
    held = add(sums0[0], [], (0,), kinds, sums0[1])
    held = add(sums12[0], held, (1, 2), kinds, sums12[1])
    held = add(both3, held, (3,), kinds, others3)
    blocks = [own, slot1, slot2, third]
    while len(blocks) < col_count:
        blocks += [exchange(w, len(blocks)) for w in blocks]
    for k in range(4, col_count):
        held = add(first(near, far_parts([blocks[k]]), [blocks[k]])[0], held, (k,), kinds)
    key_rows, value_rows = held
    return (key_rows, value_rows)


def solution(mesh):
    placed = (P(("dp", "row", "col"), None), P(), P("row", "col"), P("row", "col"))
    return jax.shard_map(
        body,
        mesh=mesh,
        in_specs=placed,
        out_specs=(P(("dp", "row", "col"), None), P(("dp", "row", "col"), None)),
        check_vma=False,
    )
```

```python
import functools

import jax
import jax.numpy as jnp
from jax import lax
from jax.experimental import pallas as pl
from jax.experimental.pallas import tpu as pltpu
from jax.sharding import PartitionSpec as P

HEAD = 128


rope_base = 500000.0


def rotation(positions):
    half_head = HEAD // 2
    frequency = rope_base ** (-2.0 * jnp.arange(half_head, dtype=jnp.float32) / HEAD)
    angles = positions.astype(jnp.float32)[:, None] * frequency[None, :]
    cosine = jnp.cos(angles)
    sine = jnp.sin(angles)
    return (
        jnp.concatenate([cosine, cosine], axis=1),
        jnp.concatenate([-sine, sine], axis=1),
    )


def params():
    return pltpu.CompilerParams(vmem_limit_bytes=24 * 1024 * 1024)


def norm_kernel(tokens_hbm, gain_hbm, out_ref, tokens, gain, sems, *, row_count, pair_count, part):
    step = norm_step(tokens_hbm.shape[0])
    blocks = [
        (d * row_count + r, r * pair_count + d)
        for r in range(row_count)
        for d in range(pair_count)
    ]
    copies = [pltpu.make_async_copy(gain_hbm, gain, sems.at[0])]
    for i in range(tokens_hbm.shape[0] // step):
        rows = pl.ds(i * step, step)
        copies.append(
            pltpu.make_async_copy(tokens_hbm.at[rows], tokens.at[rows], sems.at[1 + i])
        )
    for copy in copies:
        copy.start()
    copies[0].wait()
    for i, copy in enumerate(copies[1:]):
        copy.wait()
        rows = pl.ds(i * step, step)

        def piece(k):
            return tokens[rows, k * part : (k + 1) * part].astype(jnp.float32)

        squares = jnp.zeros((step, 128), jnp.float32)
        for _, k in blocks:
            square = piece(k) * piece(k)
            for j in range(0, part, 128):
                squares = squares + square[:, j : j + 128]
        mean = jnp.sum(squares, axis=1, keepdims=True) / (len(blocks) * part)
        inverse_rms = lax.rsqrt(mean + 1e-05)
        for place, k in blocks:
            scaled = piece(k) * inverse_rms * gain[:, k * part : (k + 1) * part]
            out_ref[place, rows, :] = scaled.astype(jnp.bfloat16)


def norm_step(rows):
    return min(32, rows)


def normalise(tokens, norm_gain, row_count, pair_count, part):
    rows, features = tokens.shape
    anywhere = pl.BlockSpec(memory_space=pl.ANY)
    return pl.pallas_call(
        functools.partial(
            norm_kernel, row_count=row_count, pair_count=pair_count, part=part
        ),
        in_specs=[anywhere, anywhere],
        out_specs=pl.BlockSpec(memory_space=pltpu.VMEM),
        out_shape=pltpu.VMEM((row_count * pair_count, rows, part), jnp.bfloat16),
        scratch_shapes=[
            pltpu.VMEM((rows, features), jnp.bfloat16),
            pltpu.VMEM((1, features), jnp.float32),
            pltpu.SemaphoreType.DMA((1 + rows // norm_step(rows),)),
        ],
        compiler_params=params(),
        name="norm",
    )(tokens, norm_gain[None, :])


def own_kernel(tile_ref, weights_ref, near_rows, far_rows, near_ref, far_ref, weights, sems, *, pair_count, row_count):
    rows = tile_ref.shape[1]
    copies = [pltpu.make_async_copy(weights_ref, weights, sems.at[2, 0])]
    halves = (near_rows, far_rows)
    for odd in (1, 0):
        for k in range(row_count // 2 * pair_count):
            pair = lax.rem(lax.axis_index("dp"), pair_count) ^ (k % pair_count)
            row = lax.axis_index("row") ^ ((k // pair_count) * 2 + odd)
            copies.append(
                pltpu.make_async_copy(
                    tile_ref.at[pair * row_count + row],
                    halves[odd].at[pl.ds(k * rows, rows)],
                    sems.at[odd, k],
                )
            )
    for copy in copies:
        copy.start()
    for copy in copies:
        copy.wait()
    for half, out_ref in ((far_rows, far_ref), (near_rows, near_ref)):
        product = jnp.dot(half[...], weights[...], preferred_element_type=jnp.float32)
        out_ref[...] = product.reshape(out_ref.shape).astype(out_ref.dtype)


def project_own(tile, weights, pair_count, row_count):
    count, rows, part = tile.shape
    chips = count // 2
    n = weights.shape[1]
    vmem = pl.BlockSpec(memory_space=pltpu.VMEM)
    half = pltpu.HBM((chips * rows, part), jnp.bfloat16)
    return pl.pallas_call(
        functools.partial(own_kernel, pair_count=pair_count, row_count=row_count),
        in_specs=[pl.BlockSpec(memory_space=pl.ANY)] * 2,
        out_specs=[vmem] * 4,
        out_shape=[
            half,
            half,
            pltpu.VMEM((chips, rows, n), jnp.bfloat16),
            pltpu.VMEM((chips, rows, n), jnp.bfloat16),
        ],
        scratch_shapes=[
            pltpu.VMEM(weights.shape, jnp.bfloat16),
            pltpu.SemaphoreType.DMA((3, chips)),
        ],
        compiler_params=params(),
        name="project_own",
    )(tile, weights)


def pair_kernel(near_hbm, far_hbm, *refs, count):
    blocks, (near_ref, far_ref) = refs[:count], refs[count : count + 2]
    near, far, weights, sems = refs[count + 2 :]
    n = weights.shape[2]
    copies = [pltpu.make_async_copy(far_hbm, far, sems.at[0])]
    copies += [
        pltpu.make_async_copy(block, weights.at[i], sems.at[2 + i])
        for i, block in enumerate(blocks)
    ]
    copies.append(pltpu.make_async_copy(near_hbm, near, sems.at[1]))
    for copy in copies:
        copy.start()

    def write(rows, out_ref, i):
        product = jnp.dot(rows[...], weights[i], preferred_element_type=jnp.float32)
        shape = out_ref.shape[:2] + (n,)
        out_ref[:, :, i * n : (i + 1) * n] = product.reshape(shape).astype(out_ref.dtype)

    copies[0].wait()
    for i in range(count):
        copies[1 + i].wait()
        write(far, far_ref, i)
    copies[-1].wait()
    for i in range(count):
        write(near, near_ref, i)


def project_both(near, far, blocks, rows):
    part, n = blocks[0].shape
    count = len(blocks)
    chips = near.shape[0] // rows
    vmem = pl.BlockSpec(memory_space=pltpu.VMEM)
    out = pltpu.VMEM((chips, rows, n * count), jnp.bfloat16)
    return pl.pallas_call(
        functools.partial(pair_kernel, count=count),
        in_specs=[pl.BlockSpec(memory_space=pl.ANY)] * (2 + count),
        out_specs=[vmem, vmem],
        out_shape=[out, out],
        scratch_shapes=[
            pltpu.VMEM(near.shape, jnp.bfloat16),
            pltpu.VMEM(far.shape, jnp.bfloat16),
            pltpu.VMEM((count, part, n), jnp.bfloat16),
            pltpu.SemaphoreType.DMA((2 + count,)),
        ],
        compiler_params=pltpu.CompilerParams(vmem_limit_bytes=58 * 1024 * 1024),
        name="project_both",
    )(near, far, *blocks)


def sum_kernel(*refs, terms, slots, kinds, width, held):
    cosine_ref, sine_ref = refs[terms : terms + 2]
    first_out = terms + 2 + held
    out_refs = refs[first_out : first_out + len(kinds)]
    blocks_ref, sems = refs[first_out + len(kinds) :]
    copies = []
    for s, slot in enumerate(slots):
        for i, kind in enumerate(kinds):
            at = (s * len(kinds) + i) * width
            block = refs[0][0, :, at : at + width].astype(jnp.float32)
            for ref in refs[1:terms]:
                block = block + ref[:, at : at + width].astype(jnp.float32)
            if kind == "key":
                turned = []
                for h in range(0, width, HEAD):
                    head = block[:, h : h + HEAD]
                    other = pltpu.roll(head, HEAD // 2, 1)
                    turned.append(head * cosine_ref[...] + other * sine_ref[...])
                block = jnp.concatenate(turned, axis=1)
            blocks_ref[s, i] = block.astype(jnp.bfloat16)
            column = pl.multiple_of((lax.axis_index("col") ^ slot) * width, width)
            copy = pltpu.make_async_copy(
                blocks_ref.at[s, i], out_refs[i].at[:, pl.ds(column, width)], sems.at[s, i]
            )
            copy.start()
            copies.append(copy)
    for copy in copies:
        copy.wait()


def finish(both, others, tables, held, slots, kinds, width, columns):
    rows = both.shape[1]
    arrays = [both, *others, *tables]
    vmem = pl.BlockSpec(memory_space=pltpu.VMEM)
    specs = [vmem] * len(arrays) + [pl.BlockSpec(memory_space=pl.ANY)] * len(held)
    return pl.pallas_call(
        functools.partial(
            sum_kernel,
            terms=1 + len(others),
            slots=slots,
            kinds=kinds,
            width=width,
            held=len(held),
        ),
        in_specs=specs,
        out_specs=[pl.BlockSpec(memory_space=pl.ANY)] * len(kinds),
        out_shape=[jax.ShapeDtypeStruct((rows, columns), jnp.bfloat16)] * len(kinds),
        scratch_shapes=[
            pltpu.VMEM((len(slots), len(kinds), rows, width), jnp.bfloat16),
            pltpu.SemaphoreType.DMA((len(slots), len(kinds))),
        ],
        input_output_aliases={len(arrays) + i: i for i in range(len(held))},
        compiler_params=params(),
        name="finish",
    )(*arrays, *held)


def body(tokens, norm_gain, w_key, w_value):
    dp_count = lax.axis_size("dp")
    row_count = lax.axis_size("row")
    col_count = lax.axis_size("col")
    dp_index = lax.axis_index("dp")
    row_index = lax.axis_index("row")
    col_index = lax.axis_index("col")
    own_rows = tokens.shape[0]
    block, width = w_key.shape
    columns = width * col_count
    pair_count = 2 if dp_count % 2 == 0 else 1
    pair_index = dp_index % pair_count
    part = block // pair_count
    inner = ((col_index + 1) % 4) // 2

    def swap(array, row_bits, pair_bits):
        pairs = []
        for d in range(dp_count):
            for r in range(row_count):
                target = (d ^ pair_bits) * row_count + (r ^ row_bits)
                pairs.append((d * row_count + r, target))
        return lax.ppermute(array, ("dp", "row"), pairs)

    def exchange(array, bits, places=(0, 1, 2, 3)):
        return lax.ppermute(
            array, "col", [(i, i ^ bits) for i in range(col_count) if i % 4 in places]
        )

    positions = (row_index * col_count + col_index) * own_rows + jnp.arange(
        own_rows, dtype=jnp.int32
    )
    tables = rotation(positions)

    always = col_index < col_count

    def stage(work, *args):
        shapes = jax.eval_shape(work, *args)

        def skip(*args):
            return jax.tree.map(lambda s: jnp.zeros(s.shape, s.dtype), shapes)

        return lax.cond(always, work, skip, *args)

    start = pair_index * part
    own = jnp.concatenate(
        [lax.dynamic_slice_in_dim(w, start, part, 0) for w in (w_key, w_value)], axis=1
    )
    slot2 = exchange(own, 2)
    slot1 = exchange(own, 1)
    chips = [(r, d) for r in range(0, row_count, 2) for d in range(pair_count)]
    (tokens, own) = lax.optimization_barrier((tokens, own))
    def spread(tokens):
        parts = normalise(tokens, norm_gain, row_count, pair_count, part)
        groups = [
            [(g * pair_count + d) * row_count + r for d in range(pair_count) for r in range(row_count)]
            for g in range(dp_count // pair_count)
        ]
        return lax.all_to_all(
            parts,
            ("dp", "row"),
            split_axis=0,
            concat_axis=0,
            tiled=True,
            axis_index_groups=groups if len(groups) > 1 else None,
        )

    tile = stage(spread, tokens)

    shape = (len(chips), own_rows, -1)

    def dot(rows, weights):
        product = jnp.dot(rows, weights, preferred_element_type=jnp.float32)
        return product.reshape(shape)

    def far_parts(blocks):
        return [dot(far, w).astype(jnp.bfloat16) for w in blocks]

    def first(near, far_parts, blocks):
        others = [swap(part, 1, 0) for part in far_parts]
        return [
            (dot(near, w) + other.astype(jnp.float32)).astype(jnp.bfloat16)
            for w, other in zip(blocks, others)
        ]

    def second(both):
        return [swap(both[k], *chips[k]) for k in range(1, len(chips))]

    def add(both, held, slots, kinds, others=None):
        others = second(both) if others is None else others
        return finish(both, others, tables, held, slots, kinds, width, columns)

    kinds = ("key", "value")
    def both_cores(near_part, far_part):
        other = swap(far_part, 1, 0)
        return (near_part.astype(jnp.float32) + other.astype(jnp.float32)).astype(jnp.bfloat16)

    (tile, own) = lax.optimization_barrier((tile, own))
    near, far, near0, far0 = project_own(tile, own, pair_count, row_count)

    def sums(near_part, far_part):
        both = both_cores(near_part, far_part)
        return both[:1], second(both)

    sums0 = stage(sums, near0, far0)
    (near, far, sums0, own, slot2) = lax.optimization_barrier((near, far, sums0, own, slot2))
    middle = exchange(own, 3, (1, 2))
    outer = exchange(slot2, 1)
    near12, far12 = project_both(near, far, [slot1, slot2], own_rows)
    sums12 = stage(sums, near12, far12)
    (sums0, sums12, middle) = lax.optimization_barrier((sums0, sums12, middle))
    (outer, middle) = lax.optimization_barrier((outer, middle))
    third = lax.optimization_barrier(jnp.where(inner == 1, middle, outer))
    both3 = first(near, far_parts([third]), [third])[0]
    others3 = second(both3)
    held = add(sums0[0], [], (0,), kinds, sums0[1])
    held = add(sums12[0], held, (1, 2), kinds, sums12[1])
    held = add(both3, held, (3,), kinds, others3)
    blocks = [own, slot1, slot2, third]
    while len(blocks) < col_count:
        blocks += [exchange(w, len(blocks)) for w in blocks]
    for k in range(4, col_count):
        held = add(first(near, far_parts([blocks[k]]), [blocks[k]])[0], held, (k,), kinds)
    key_rows, value_rows = held
    return (key_rows, value_rows)


def solution(mesh):
    placed = (P(("dp", "row", "col"), None), P(), P("row", "col"), P("row", "col"))
    return jax.shard_map(
        body,
        mesh=mesh,
        in_specs=placed,
        out_specs=(P(("dp", "row", "col"), None), P(("dp", "row", "col"), None)),
        check_vma=False,
    )
```
